32 devices in a mesh: parts: 2 (over y), blk: 16 (over z, x, core).
Axes of the slice: x: 2, y: 2, z: 4, core: 2. Of those that a mesh axis runs over, the one named last changes fastest.
Arguments:
- emb: bfloat16 [4096, 1024], P(('parts', 'blk')), parts along dimension 0, may hold values from -11 to 11
- cluster: int32 [4096], P(('parts', 'blk')), parts along dimension 0, may hold values from 0 to 3, as said below
Outputs:
- neighbour_mean: bfloat16 [4096, 1024], P(('parts', 'blk')), parts along dimension 0
- dup_score: float32 [4096], P(('parts', 'blk')), parts along dimension 0
The draws below stay inside these ranges and needn't reach their ends.
There are 2 independent parts, one for each index of `parts`. The reference program is written for one: setup_inputs(seed, part) draws one part's arguments, and reference() takes and returns one part's arrays. A program takes and returns all parts, laid end to end along the dimension named above; each array names one. Nothing has to cross between parts.
Inputs may be any that keep to these rules, and one draw needn't show every extreme that they name: `cluster`: clusters r * 4 to r * 4 + 3 form group r. Among the rows of one device (aligned blocks of 128 rows) at most 128 lie in one group's clusters; in every draw one group has exactly 128 rows on every device.
All inputs are finite; a program needn't handle non-finite values.
Results may differ from the reference program's by a relative error of at most 0.0022.
Values may be sent and summed in bfloat16 or wider, within the bound.
A program may use at most 64 MiB of HBM per device.

```python
import math
import jax
import jax.numpy as jnp
from jax import lax

D = 1024
CL_CYCLE = 4
DOC_DEV = 128
GROUPS = 1
RMAX = 128
NCLUS = 4
DOCS = 2048


def cluster_draw(key):
    base_key = jax.random.fold_in(key, 7)
    heavy_key, device_key, local_key = jax.random.split(base_key, 3)
    heavy_group = jax.random.randint(heavy_key, (), 0, GROUPS)
    label_count = GROUPS * RMAX
    labels = jnp.arange(label_count, dtype=jnp.int32)

    def device_labels(one_key):
        label_key, row_key = jax.random.split(one_key)
        shuffled = jax.random.permutation(label_key, label_count).astype(jnp.int32)
        priority = jnp.where(labels < RMAX, -1, shuffled)
        chosen = jnp.argsort(priority, stable=True)[:DOC_DEV].astype(jnp.int32)
        owner = (chosen // RMAX + heavy_group) % GROUPS
        return owner[jax.random.permutation(row_key, DOC_DEV)]
    owners = jax.vmap(device_labels)(jax.random.split(device_key, DOCS // DOC_DEV)).reshape(DOCS)
    local_id = jax.random.randint(local_key, (DOCS,), 0, CL_CYCLE)
    return (owners * CL_CYCLE + local_id).astype(jnp.int32)


def draw_cluster(key, part):
    return cluster_draw(key)


def draw_emb(key, part):
    clusters = cluster_draw(key)
    key = jax.random.fold_in(key, 11)
    center_key, anchor_key, family_key, spread_key, jitter_key = jax.random.split(key, 5)
    families = max(4, DOCS // (NCLUS * 20))
    centers = jax.random.truncated_normal(center_key, -4.0, 4.0, (NCLUS, D), jnp.float32)
    anchors = jax.random.truncated_normal(anchor_key, -4.0, 4.0, (NCLUS * families, D), jnp.float32)
    family = jax.random.randint(family_key, (DOCS,), 0, families)
    spread = jnp.exp(jax.random.uniform(spread_key, (DOCS, 1), jnp.float32, math.log(0.15), math.log(0.8)))
    jitter = jax.random.truncated_normal(jitter_key, -4.0, 4.0, (DOCS, D), jnp.float32)
    values = 0.6 * centers[clusters] + 1.2 * anchors[clusters * families + family] + spread * jitter
    return values.astype(jnp.bfloat16)


def setup_inputs(seed: int = 0, part: int = 0) -> dict:
    seeds = jax.random.split(jax.random.key(seed), 3)
    own_keys = jax.random.split(jax.random.fold_in(seeds[2], part), 3)
    emb = draw_emb(jax.random.fold_in(jax.random.fold_in(seeds[2], part), 71), part)
    cluster = draw_cluster(jax.random.fold_in(jax.random.fold_in(seeds[2], part), 71), part)
    return dict(emb=emb, cluster=cluster)


SHARPNESS = 2.0


def reference(emb, cluster):
    order = jnp.argsort(cluster, stable=True).astype(jnp.int32)
    rows = emb[order].astype(jnp.float32)
    sorted_ids = cluster[order].astype(jnp.int32)
    norms = jnp.sum(rows * rows, 1)
    span = math.gcd(DOCS, 512)
    count = DOCS // span
    block_table = sorted_ids.reshape(count, span)
    lowest = block_table[:, 0]
    highest = block_table[:, span - 1]

    def per_row(row_block):
        first = row_block * span
        own_rows = lax.dynamic_slice_in_dim(rows, first, span, 0)
        own_norm = lax.dynamic_slice_in_dim(norms, first, span, 0)
        own_ids = lax.dynamic_slice_in_dim(sorted_ids, first, span, 0)
        own_pos = first + jnp.arange(span, dtype=jnp.int32)

        def per_col(carry, col_block):
            start = col_block * span

            def work(state):
                pulled, totals = state
                far_rows = lax.dynamic_slice_in_dim(rows, start, span, 0)
                far_norm = lax.dynamic_slice_in_dim(norms, start, span, 0)
                far_ids = lax.dynamic_slice_in_dim(sorted_ids, start, span, 0)
                far_pos = start + jnp.arange(span, dtype=jnp.int32)
                inner = jnp.dot(own_rows, far_rows.T, precision=lax.Precision.HIGHEST)
                distance = jnp.maximum(own_norm[:, None] + far_norm[None, :] - 2.0 * inner, 0.0)
                allowed = (own_ids[:, None] == far_ids[None, :]) & (own_pos[:, None] != far_pos[None, :])
                weight = jnp.where(allowed, jnp.exp(-SHARPNESS * distance / D), 0.0)
                rounded = lax.optimization_barrier(weight.astype(jnp.bfloat16)).astype(jnp.float32)
                pulled = pulled + jnp.dot(rounded, far_rows, precision=lax.Precision.HIGHEST)
                return pulled, totals + jnp.sum(weight, 1)

            def unchanged(state):
                return state

            intersection = (lowest[col_block] <= highest[row_block]) & (lowest[row_block] <= highest[col_block])
            return lax.cond(intersection, work, unchanged, carry), None

        start_state = (jnp.zeros((span, D), jnp.float32), jnp.zeros((span,), jnp.float32))
        (pulled, totals), _ = lax.scan(per_col, start_state, jnp.arange(count, dtype=jnp.int32))
        return pulled, totals

    pulled, totals = lax.map(per_row, jnp.arange(count, dtype=jnp.int32))
    pulled = jnp.zeros((DOCS, D), jnp.float32).at[order].set(pulled.reshape(DOCS, D))
    totals = jnp.zeros((DOCS,), jnp.float32).at[order].set(totals.reshape(DOCS))
    neighbour_mean = (pulled / (1.0 + totals)[:, None]).astype(jnp.bfloat16)
    dup_score = jnp.log(1.0 + totals)
    return neighbour_mean, dup_score
```

```python
import jax
import jax.numpy as jnp
from jax import lax
from jax.experimental import pallas as pl
from jax.experimental.pallas import tpu as pltpu
from jax.sharding import PartitionSpec as P

CYCLE = 16
CL_CYCLE = 4


SHARPNESS = 2.0


def passed_along(block, axis, distance):
    devices = range(lax.axis_size(axis))
    route = [((i - distance) % len(devices), i) for i in devices]
    return lax.ppermute(block, axis, route)


def squares(rows):
    return jnp.sum(jnp.square(rows.astype(jnp.float32)), 1)


def weights(home_rows, home_norm, home_ids, visit_rows, visit_ids, skip_self):
    visit_norm = squares(visit_rows)
    inner = lax.dot_general(
        home_rows, visit_rows, (((1,), (1,)), ((), ())), preferred_element_type=jnp.float32
    )
    distance = jnp.maximum(home_norm[:, None] + visit_norm[None, :] - 2.0 * inner, 0.0)
    allowed = (home_ids[:, None] == visit_ids[None, :]) & (home_ids[:, None] >= 0)
    if skip_self:
        row_pos = jnp.arange(home_rows.shape[0], dtype=jnp.int32)
        allowed = allowed & (row_pos[:, None] != row_pos[None, :])
    return jnp.where(allowed, jnp.exp(-SHARPNESS * distance / home_rows.shape[1]), 0.0)


def absorb(weight, visit_rows, pulled, totals):
    pulled = pulled + jnp.dot(
        weight.astype(jnp.bfloat16), visit_rows, preferred_element_type=jnp.float32
    )
    return (pulled, totals + jnp.sum(weight, 1))


def local(emb, cluster):
    devices = lax.axis_size("blk")
    groups = devices // CYCLE
    doc_rows, width = emb.shape
    capacity = min(doc_rows // CYCLE, 3 * doc_rows // (2 * CYCLE * groups))
    slots = devices * capacity
    group_of = cluster // CL_CYCLE
    member = (group_of[:, None] == jnp.arange(groups, dtype=jnp.int32)[None, :]).astype(jnp.int32)
    running = jnp.cumsum(member, 0) - member
    place = jnp.sum(running * member, 1)
    target = place % CYCLE * groups + group_of
    slot_index = target * capacity + place // CYCLE
    send_rows = jnp.zeros((slots, width), jnp.bfloat16).at[slot_index].set(emb)
    send_ids = jnp.full((slots,), -1, jnp.int32).at[slot_index].set(cluster)
    got_rows, got_ids = (
        lax.all_to_all(
            send_rows.reshape(devices, capacity, width),
            "blk",
            split_axis=0,
            concat_axis=0,
            tiled=True,
        ),
        lax.all_to_all(
            send_ids.reshape(devices, capacity), "blk", split_axis=0, concat_axis=0, tiled=True
        ),
    )
    home_rows = got_rows.reshape(slots, width)
    home_ids = got_ids.reshape(slots)
    home_norm = squares(home_rows)
    pulled = jnp.zeros((slots, width), jnp.float32)
    totals = jnp.zeros((slots,), jnp.float32)
    weight = weights(home_rows, home_norm, home_ids, home_rows, home_ids, True)
    pulled, totals = absorb(weight, home_rows, pulled, totals)

    def advance(step, carry):
        visit_rows, visit_ids, pulled, totals = carry
        visit_rows, visit_ids = passed_along((visit_rows, visit_ids), "blk", groups)
        weight = weights(home_rows, home_norm, home_ids, visit_rows, visit_ids, False)
        pulled, totals = absorb(weight, visit_rows, pulled, totals)
        return (visit_rows, visit_ids, pulled, totals)

    _, _, pulled, totals = lax.fori_loop(1, CYCLE, advance, (home_rows, home_ids, pulled, totals))
    back_pulled, back_totals = (
        lax.all_to_all(
            pulled.reshape(devices, capacity, width), "blk", split_axis=0, concat_axis=0, tiled=True
        ),
        lax.all_to_all(
            totals.reshape(devices, capacity), "blk", split_axis=0, concat_axis=0, tiled=True
        ),
    )
    own_pulled = back_pulled.reshape(slots, width)[slot_index]
    own_totals = back_totals.reshape(slots)[slot_index]
    neighbour_mean = (own_pulled / (1.0 + own_totals)[:, None]).astype(jnp.bfloat16)
    dup_score = jnp.log(1.0 + own_totals)
    return (neighbour_mean, dup_score)


PIECES = 2
GATHER_DEVICES = 16
MESH = pl.DeviceIdType.MESH


def gather_kernel(emb_ref, ids_ref, mean_ref, score_ref, docs, meta, pulled, totals,
                  send_sem, recv_sem, meta_send, meta_recv):
    rows, width = emb_ref.shape
    piece = rows // PIECES
    me = lax.axis_index("blk")
    z, x, core = me // 4, (me // 2) % 2, me % 2
    z_end = GATHER_DEVICES // 4 - 1

    def slot_of(zz, xx, cc):
        return zz * 4 + xx * 2 + cc

    barrier = pltpu.get_barrier_semaphore()
    for step in range(1, GATHER_DEVICES):
        pl.semaphore_signal(
            barrier, inc=1, device_id={"blk": (me + step) % GATHER_DEVICES}, device_id_type=MESH
        )

    own = emb_ref[...]
    for h in range(PIECES):
        docs[me, h] = own[h * piece:(h + 1) * piece]
    own_f = own.astype(jnp.float32)
    own_norm = jnp.sum(own_f * own_f, 1, keepdims=True)
    line = lax.broadcasted_iota(jnp.int32, (rows, rows), 0)
    lane = lax.broadcasted_iota(jnp.int32, (rows, rows), 1)
    diagonal = line == lane
    ids_row = ids_ref[...].astype(jnp.float32)
    own_ids = jnp.sum(jnp.where(diagonal, ids_row, 0.0), 1, keepdims=True)
    norm_row = jnp.sum(jnp.where(diagonal, own_norm, 0.0), 0, keepdims=True)
    meta_line = lax.broadcasted_iota(jnp.int32, (8, rows), 0)
    meta[me] = jnp.where(meta_line == 0, norm_row, ids_row)
    pulled[...] = jnp.zeros_like(pulled)
    totals[...] = jnp.zeros_like(totals)

    pl.semaphore_wait(barrier, GATHER_DEVICES - 1)

    sent = []

    def copy(way, slot, h, target):
        return pltpu.make_async_remote_copy(
            src_ref=docs.at[slot, h],
            dst_ref=docs.at[slot, h],
            send_sem=send_sem.at[way, slot, h],
            recv_sem=recv_sem.at[slot, h],
            device_id={"blk": target},
            device_id_type=MESH,
        )

    def send(pred, way, slot, h):
        target = {
            "up": slot_of(jnp.minimum(z + 1, z_end), x, core),
            "down": slot_of(jnp.maximum(z - 1, 0), x, core),
            "x": slot_of(z, 1 - x, core),
            "core": slot_of(z, x, 1 - core),
        }[way]
        index = ("up", "down", "x", "core").index(way)

        def start():
            copy(index, slot, h, target).start()

        def finish():
            copy(index, slot, h, target).wait_send()

        if pred is None:
            start()
            sent.append(finish)
        else:
            pl.when(pred)(start)
            sent.append(lambda: pl.when(pred)(finish))

    def arrive(slot, h):
        copy(3, slot, h, slot_of(z, x, 1 - core)).wait_recv()

    def pass_column(zz, h, wait):
        slot = slot_of(zz, x, core)
        if wait:
            arrive(slot, h)
        send((zz >= z) & (z > 0), "down", slot, h)
        send((zz <= z) & (z < z_end), "up", slot, h)
        beside = ((z == 1) & (zz == 0)) | ((z == z_end - 1) & (zz == z_end))
        far = ((z == 0) & (zz == z_end)) | ((z == z_end) & (zz == 0))
        skip = (beside | far) if h < PIECES // 2 else beside
        send(jnp.logical_not(skip), "x", slot, h)
        send(None, "core", slot, h)

    def pass_other(zz, h):
        slot = slot_of(zz, 1 - x, core)
        arrive(slot, h)
        up = (z == 0) & (zz == 0)
        down = (z == z_end) & (zz == z_end)
        if h < PIECES // 2:
            up = up | ((z == z_end - 1) & (zz == 0))
            down = down | ((z == 1) & (zz == z_end))
        send(down, "down", slot, h)
        send(up, "up", slot, h)
        send(None, "core", slot, h)

    def meta_copy(step):
        target = (me + step) % GATHER_DEVICES
        return pltpu.make_async_remote_copy(
            src_ref=meta.at[me],
            dst_ref=meta.at[me],
            send_sem=meta_send.at[step],
            recv_sem=meta_recv.at[me],
            device_id={"blk": target},
            device_id_type=MESH,
        )

    def meta_arrive(step):
        source = (me + step) % GATHER_DEVICES
        pltpu.make_async_remote_copy(
            src_ref=meta.at[source],
            dst_ref=meta.at[source],
            send_sem=meta_send.at[step],
            recv_sem=meta_recv.at[source],
            device_id={"blk": source},
            device_id_type=MESH,
        ).wait_recv()

    def absorb(zz, xx, own_chip=False):
        for h in range(PIECES):
            arrive(slot_of(zz, xx, 1 - core), h)
        first = slot_of(zz, xx, 0)
        visit = docs[pl.ds(first, 2)].reshape(2 * rows, width)
        info = meta[pl.ds(first, 2)]
        visit_norm = jnp.concatenate([info[0, 0:1], info[1, 0:1]], 1)
        visit_ids = jnp.concatenate([info[0, 1:2], info[1, 1:2]], 1)
        inner = lax.dot_general(
            emb_ref[...], visit, (((1,), (1,)), ((), ())), preferred_element_type=jnp.float32
        )
        distance = jnp.maximum(own_norm + visit_norm - 2.0 * inner, 0.0)
        allowed = own_ids == visit_ids
        if own_chip:
            home = lax.broadcasted_iota(jnp.int32, (rows, 2 * rows), 0) + core * rows
            away = lax.broadcasted_iota(jnp.int32, (rows, 2 * rows), 1)
            allowed = allowed & (home != away)
        weight = jnp.where(allowed, jnp.exp(distance * (-SHARPNESS / width)), 0.0)
        totals[...] += jnp.sum(weight, 1, keepdims=True)
        pulled[...] += jnp.dot(
            weight.astype(jnp.bfloat16), visit, preferred_element_type=jnp.float32
        )

    z1 = jnp.where(z % 2 == 0, 1, 2)
    z3 = jnp.where(z < 2, z_end, 0)
    z2 = 6 - z - z1 - z3
    halves = range(PIECES)

    for h in halves:
        pass_column(z, h, False)
    for step in range(1, GATHER_DEVICES):
        meta_copy(step).start()
    for step in range(1, GATHER_DEVICES):
        meta_arrive(step)
    absorb(z, x, True)
    for h in halves:
        pass_column(z1, h, True)
    for h in halves:
        pass_other(z, h)
    absorb(z1, x)
    absorb(z, 1 - x)
    for h in halves:
        pass_column(z2, h, True)
    absorb(z2, x)
    for h in halves:
        if h < PIECES // 2:
            pass_column(z3, h, True)
    for h in halves:
        pass_other(z1, h)
    for h in halves:
        if h >= PIECES // 2:
            pass_column(z3, h, True)
    absorb(z1, 1 - x)
    absorb(z3, x)
    for h in halves:
        pass_other(z2, h)
    absorb(z2, 1 - x)
    for h in halves:
        pass_other(z3, h)
    absorb(z3, 1 - x)

    scale = 1.0 + totals[...]
    mean_ref[...] = (pulled[...] / scale).astype(jnp.bfloat16)
    score_ref[...] = jnp.sum(jnp.where(diagonal, jnp.log(scale), 0.0), 0, keepdims=True)
    for finish in sent:
        finish()
    for step in range(1, GATHER_DEVICES):
        meta_copy(step).wait_send()


def gathered(emb, cluster):
    rows, width = emb.shape
    devices = GATHER_DEVICES
    vmem = pl.BlockSpec(memory_space=pltpu.VMEM)
    mean, score = pl.pallas_call(
        gather_kernel,
        out_shape=(
            jax.ShapeDtypeStruct((rows, width), jnp.bfloat16),
            jax.ShapeDtypeStruct((1, rows), jnp.float32),
        ),
        in_specs=[vmem, vmem],
        out_specs=(vmem, vmem),
        scratch_shapes=[
            pltpu.VMEM((devices, PIECES, rows // PIECES, width), jnp.bfloat16),
            pltpu.VMEM((devices, 8, rows), jnp.float32),
            pltpu.VMEM((rows, width), jnp.float32),
            pltpu.VMEM((rows, 1), jnp.float32),
            pltpu.SemaphoreType.DMA((4, devices, PIECES)),
            pltpu.SemaphoreType.DMA((devices, PIECES)),
            pltpu.SemaphoreType.DMA((devices,)),
            pltpu.SemaphoreType.DMA((devices,)),
        ],
        compiler_params=pltpu.CompilerParams(
            collective_id=0, has_side_effects=True, vmem_limit_bytes=40 << 20
        ),
        cost_estimate=pl.CostEstimate(
            flops=4 * devices * rows * rows * width,
            bytes_accessed=4 * rows * width,
            transcendentals=devices * rows * rows,
        ),
    )(emb, cluster.reshape(1, rows))
    return mean, score.reshape(rows)


def solution(mesh):
    small = mesh.shape["blk"] == GATHER_DEVICES
    return jax.shard_map(
        gathered if small else local,
        mesh=mesh,
        in_specs=(P(("parts", "blk"), None), P(("parts", "blk"))),
        out_specs=(P(("parts", "blk"), None), P(("parts", "blk"))),
        check_vma=False,
    )
```

```python
import jax
import jax.numpy as jnp
from jax import lax
from jax.experimental import pallas as pl
from jax.experimental.pallas import tpu as pltpu
from jax.sharding import PartitionSpec as P

CYCLE = 16
CL_CYCLE = 4


SHARPNESS = 2.0


def passed_along(block, axis, distance):
    devices = range(lax.axis_size(axis))
    route = [((i - distance) % len(devices), i) for i in devices]
    return lax.ppermute(block, axis, route)


def squares(rows):
    return jnp.sum(jnp.square(rows.astype(jnp.float32)), 1)


def weights(home_rows, home_norm, home_ids, visit_rows, visit_ids, skip_self):
    visit_norm = squares(visit_rows)
    inner = lax.dot_general(
        home_rows, visit_rows, (((1,), (1,)), ((), ())), preferred_element_type=jnp.float32
    )
    distance = jnp.maximum(home_norm[:, None] + visit_norm[None, :] - 2.0 * inner, 0.0)
    allowed = (home_ids[:, None] == visit_ids[None, :]) & (home_ids[:, None] >= 0)
    if skip_self:
        row_pos = jnp.arange(home_rows.shape[0], dtype=jnp.int32)
        allowed = allowed & (row_pos[:, None] != row_pos[None, :])
    return jnp.where(allowed, jnp.exp(-SHARPNESS * distance / home_rows.shape[1]), 0.0)


def absorb(weight, visit_rows, pulled, totals):
    pulled = pulled + jnp.dot(
        weight.astype(jnp.bfloat16), visit_rows, preferred_element_type=jnp.float32
    )
    return (pulled, totals + jnp.sum(weight, 1))


def local(emb, cluster):
    devices = lax.axis_size("blk")
    groups = devices // CYCLE
    doc_rows, width = emb.shape
    capacity = min(doc_rows // CYCLE, 3 * doc_rows // (2 * CYCLE * groups))
    slots = devices * capacity
    group_of = cluster // CL_CYCLE
    member = (group_of[:, None] == jnp.arange(groups, dtype=jnp.int32)[None, :]).astype(jnp.int32)
    running = jnp.cumsum(member, 0) - member
    place = jnp.sum(running * member, 1)
    target = place % CYCLE * groups + group_of
    slot_index = target * capacity + place // CYCLE
    send_rows = jnp.zeros((slots, width), jnp.bfloat16).at[slot_index].set(emb)
    send_ids = jnp.full((slots,), -1, jnp.int32).at[slot_index].set(cluster)
    got_rows, got_ids = (
        lax.all_to_all(
            send_rows.reshape(devices, capacity, width),
            "blk",
            split_axis=0,
            concat_axis=0,
            tiled=True,
        ),
        lax.all_to_all(
            send_ids.reshape(devices, capacity), "blk", split_axis=0, concat_axis=0, tiled=True
        ),
    )
    home_rows = got_rows.reshape(slots, width)
    home_ids = got_ids.reshape(slots)
    home_norm = squares(home_rows)
    pulled = jnp.zeros((slots, width), jnp.float32)
    totals = jnp.zeros((slots,), jnp.float32)
    weight = weights(home_rows, home_norm, home_ids, home_rows, home_ids, True)
    pulled, totals = absorb(weight, home_rows, pulled, totals)

    def advance(step, carry):
        visit_rows, visit_ids, pulled, totals = carry
        visit_rows, visit_ids = passed_along((visit_rows, visit_ids), "blk", groups)
        weight = weights(home_rows, home_norm, home_ids, visit_rows, visit_ids, False)
        pulled, totals = absorb(weight, visit_rows, pulled, totals)
        return (visit_rows, visit_ids, pulled, totals)

    _, _, pulled, totals = lax.fori_loop(1, CYCLE, advance, (home_rows, home_ids, pulled, totals))
    back_pulled, back_totals = (
        lax.all_to_all(
            pulled.reshape(devices, capacity, width), "blk", split_axis=0, concat_axis=0, tiled=True
        ),
        lax.all_to_all(
            totals.reshape(devices, capacity), "blk", split_axis=0, concat_axis=0, tiled=True
        ),
    )
    own_pulled = back_pulled.reshape(slots, width)[slot_index]
    own_totals = back_totals.reshape(slots)[slot_index]
    neighbour_mean = (own_pulled / (1.0 + own_totals)[:, None]).astype(jnp.bfloat16)
    dup_score = jnp.log(1.0 + own_totals)
    return (neighbour_mean, dup_score)


PIECES = 2
GATHER_DEVICES = 16
MESH = pl.DeviceIdType.MESH


def gather_kernel(emb_ref, cluster_ref, mean_ref, score_ref, docs, meta, ids_ref, pulled, totals,
                  load_sem, send_sem, recv_sem, meta_send, meta_recv):
    rows, width = emb_ref.shape
    piece = rows // PIECES
    me = lax.axis_index("blk")
    z, x, core = me // 4, (me // 2) % 2, me % 2
    z_end = GATHER_DEVICES // 4 - 1

    def slot_of(zz, xx, cc):
        return zz * 4 + xx * 2 + cc

    ways = ("up", "down", "x", "core")
    neighbour = {
        "up": slot_of(jnp.minimum(z + 1, z_end), x, core),
        "down": slot_of(jnp.maximum(z - 1, 0), x, core),
        "x": slot_of(z, 1 - x, core),
        "core": slot_of(z, x, 1 - core),
    }

    barrier = pltpu.get_barrier_semaphore()

    def greet(way):
        pl.semaphore_signal(
            barrier, inc=1, device_id={"blk": neighbour[way]}, device_id_type=MESH
        )

    pl.when(z > 0)(lambda: greet("down"))
    pl.when(z < z_end)(lambda: greet("up"))
    greet("x")
    greet("core")

    loads = [pltpu.make_async_copy(cluster_ref, ids_ref, load_sem.at[PIECES])]
    for h in range(PIECES):
        loads.append(
            pltpu.make_async_copy(
                emb_ref.at[pl.ds(h * piece, piece)], docs.at[me, h], load_sem.at[h]
            )
        )
    for load in loads:
        load.start()
    pulled[...] = jnp.zeros_like(pulled)
    totals[...] = jnp.zeros_like(totals)
    for load in loads:
        load.wait()

    own = docs[me].reshape(rows, width)
    own_f = own.astype(jnp.float32)
    own_norm = jnp.sum(own_f * own_f, 1, keepdims=True)
    line = lax.broadcasted_iota(jnp.int32, (rows, rows), 0)
    lane = lax.broadcasted_iota(jnp.int32, (rows, rows), 1)
    diagonal = line == lane
    ids_row = ids_ref[...].astype(jnp.float32)
    own_ids = jnp.sum(jnp.where(diagonal, ids_row, 0.0), 1, keepdims=True)
    norm_row = jnp.sum(jnp.where(diagonal, own_norm, 0.0), 0, keepdims=True)
    meta_line = lax.broadcasted_iota(jnp.int32, (8, rows), 0)
    meta[me] = jnp.where(meta_line == 0, norm_row, ids_row)

    pl.semaphore_wait(barrier, jnp.where((z > 0) & (z < z_end), 4, 3))

    sent = []

    def copy(way, slot, h, target):
        return pltpu.make_async_remote_copy(
            src_ref=docs.at[slot, h],
            dst_ref=docs.at[slot, h],
            send_sem=send_sem.at[way, slot, h],
            recv_sem=recv_sem.at[slot, h],
            device_id={"blk": target},
            device_id_type=MESH,
        )

    def meta_copy(way, slot, target):
        return pltpu.make_async_remote_copy(
            src_ref=meta.at[slot],
            dst_ref=meta.at[slot],
            send_sem=meta_send.at[way, slot],
            recv_sem=meta_recv.at[slot],
            device_id={"blk": target},
            device_id_type=MESH,
        )

    def send(pred, way, slot, h):
        index = ways.index(way)
        target = neighbour[way]

        def start():
            if h == PIECES - 1:
                meta_copy(index, slot, target).start()
            copy(index, slot, h, target).start()

        def finish():
            if h == PIECES - 1:
                meta_copy(index, slot, target).wait_send()
            copy(index, slot, h, target).wait_send()

        pl.when(pred)(start)
        sent.append(lambda: pl.when(pred)(finish))

    def arrive(slot, h):
        if h == PIECES - 1:
            meta_copy(3, slot, neighbour["core"]).wait_recv()
        copy(3, slot, h, neighbour["core"]).wait_recv()

    def to_line(zz, h):
        slot = slot_of(zz, x, core)
        send((zz >= z) & (z > 0), "down", slot, h)
        send((zz <= z) & (z < z_end), "up", slot, h)

    def to_side(zz, h):
        from_low, from_high = (zz == 0) & (z > 0), (zz == z_end) & (z < z_end)
        if h >= PIECES // 2:
            from_low = from_low & (z == 1)
            from_high = from_high & (z == z_end - 1)
        send(jnp.logical_not(from_low | from_high), "x", slot_of(zz, x, core), h)

    def to_core(zz, xx, h, only):
        send(only, "core", slot_of(zz, xx, core), h)

    def pass_column(zz, h):
        arrive(slot_of(zz, x, core), h)
        to_line(zz, h)
        to_side(zz, h)
        to_core(zz, x, h, always)

    def pass_other(zz, h, only):
        slot = slot_of(zz, 1 - x, core)
        pl.when(only)(lambda: arrive(slot, h))
        up, down = (zz == 0) & only, (zz == z_end) & only
        if h >= PIECES // 2:
            up, down = up & (z == 0), down & (z == z_end)
        send(down & (z > 0), "down", slot, h)
        send(up & (z < z_end), "up", slot, h)
        to_core(zz, 1 - x, h, only)

    def absorb(zz, xx, own_chip=False):
        for h in range(PIECES):
            arrive(slot_of(zz, xx, 1 - core), h)
        first = slot_of(zz, xx, 0)
        visit = docs[pl.ds(first, 2)].reshape(2 * rows, width)
        info = meta[pl.ds(first, 2)]
        visit_norm = jnp.concatenate([info[0, 0:1], info[1, 0:1]], 1)
        visit_ids = jnp.concatenate([info[0, 1:2], info[1, 1:2]], 1)
        inner = lax.dot_general(
            docs[me].reshape(rows, width),
            visit,
            (((1,), (1,)), ((), ())),
            preferred_element_type=jnp.float32,
        )
        distance = jnp.maximum(own_norm + visit_norm - 2.0 * inner, 0.0)
        allowed = own_ids == visit_ids
        if own_chip:
            home = lax.broadcasted_iota(jnp.int32, (rows, 2 * rows), 0) + core * rows
            away = lax.broadcasted_iota(jnp.int32, (rows, 2 * rows), 1)
            allowed = allowed & (home != away)
        weight = jnp.where(allowed, jnp.exp(distance * (-SHARPNESS / width)), 0.0)
        totals[...] += jnp.sum(weight, 1, keepdims=True)
        pulled[...] += jnp.dot(
            weight.astype(jnp.bfloat16), visit, preferred_element_type=jnp.float32
        )

    z1 = jnp.where(z % 2 == 0, 1, 2)
    z3 = jnp.where(z < 2, z_end, 0)
    z2 = 6 - z - z1 - z3
    early = range(PIECES // 2)
    late = range(PIECES // 2, PIECES)
    middle = (z > 0) & (z < z_end)
    end = jnp.logical_not(middle)
    always = z >= 0

    for h in (*late, *early):
        to_line(z, h)
    for h in (*early, *late):
        to_side(z, h)
    for h in (*late, *early):
        to_core(z, x, h, always)
    absorb(z, x, True)
    for h in (*late, *early):
        pass_column(z1, h)
    for h in (*early, *late):
        pass_other(z, h, always)
    absorb(z1, x)
    absorb(z, 1 - x)
    for h in (*late, *early):
        pass_column(z2, h)
    absorb(z2, x)
    for h in early:
        pass_other(z2, h, middle)
    for h in late:
        pass_column(z3, h)
    for h in (*late, *early):
        pass_other(z1, h, always)
    for h in early:
        pass_column(z3, h)
    absorb(z1, 1 - x)
    for h in late:
        pass_other(z2, h, always)
    for h in early:
        pass_other(z2, h, end)
    for h in early:
        pass_other(z3, h, middle)
    absorb(z3, x)
    absorb(z2, 1 - x)
    for h in late:
        pass_other(z3, h, always)
    for h in early:
        pass_other(z3, h, end)
    absorb(z3, 1 - x)

    scale = 1.0 + totals[...]
    mean_ref[...] = (pulled[...] / scale).astype(jnp.bfloat16)
    score_ref[...] = jnp.sum(jnp.where(diagonal, jnp.log(scale), 0.0), 0, keepdims=True)
    for finish in sent:
        finish()


def gathered(emb, cluster):
    rows, width = emb.shape
    devices = GATHER_DEVICES
    vmem = pl.BlockSpec(memory_space=pltpu.VMEM)
    mean, score = pl.pallas_call(
        gather_kernel,
        out_shape=(
            jax.ShapeDtypeStruct((rows, width), jnp.bfloat16),
            jax.ShapeDtypeStruct((1, rows), jnp.float32),
        ),
        in_specs=[pl.BlockSpec(memory_space=pl.ANY)] * 2,
        out_specs=(vmem, vmem),
        scratch_shapes=[
            pltpu.VMEM((devices, PIECES, rows // PIECES, width), jnp.bfloat16),
            pltpu.VMEM((devices, 8, rows), jnp.float32),
            pltpu.VMEM((1, rows), jnp.int32),
            pltpu.VMEM((rows, width), jnp.float32),
            pltpu.VMEM((rows, 1), jnp.float32),
            pltpu.SemaphoreType.DMA((PIECES + 1,)),
            pltpu.SemaphoreType.DMA((4, devices, PIECES)),
            pltpu.SemaphoreType.DMA((devices, PIECES)),
            pltpu.SemaphoreType.DMA((4, devices)),
            pltpu.SemaphoreType.DMA((devices,)),
        ],
        compiler_params=pltpu.CompilerParams(
            collective_id=0, has_side_effects=True, vmem_limit_bytes=40 << 20
        ),
        cost_estimate=pl.CostEstimate(
            flops=4 * devices * rows * rows * width,
            bytes_accessed=4 * rows * width,
            transcendentals=devices * rows * rows,
        ),
    )(emb, cluster.reshape(1, rows))
    return mean, score.reshape(rows)


def solution(mesh):
    small = mesh.shape["blk"] == GATHER_DEVICES
    return jax.shard_map(
        gathered if small else local,
        mesh=mesh,
        in_specs=(P(("parts", "blk"), None), P(("parts", "blk"))),
        out_specs=(P(("parts", "blk"), None), P(("parts", "blk"))),
        check_vma=False,
    )
```

```python
import jax
import jax.numpy as jnp
from jax import lax
from jax.experimental import pallas as pl
from jax.experimental.pallas import tpu as pltpu
from jax.sharding import PartitionSpec as P

CYCLE = 16
CL_CYCLE = 4


SHARPNESS = 2.0


def passed_along(block, axis, distance):
    devices = range(lax.axis_size(axis))
    route = [((i - distance) % len(devices), i) for i in devices]
    return lax.ppermute(block, axis, route)


def squares(rows):
    return jnp.sum(jnp.square(rows.astype(jnp.float32)), 1)


def weights(home_rows, home_norm, home_ids, visit_rows, visit_ids, skip_self):
    visit_norm = squares(visit_rows)
    inner = lax.dot_general(
        home_rows, visit_rows, (((1,), (1,)), ((), ())), preferred_element_type=jnp.float32
    )
    distance = jnp.maximum(home_norm[:, None] + visit_norm[None, :] - 2.0 * inner, 0.0)
    allowed = (home_ids[:, None] == visit_ids[None, :]) & (home_ids[:, None] >= 0)
    if skip_self:
        row_pos = jnp.arange(home_rows.shape[0], dtype=jnp.int32)
        allowed = allowed & (row_pos[:, None] != row_pos[None, :])
    return jnp.where(allowed, jnp.exp(-SHARPNESS * distance / home_rows.shape[1]), 0.0)


def absorb(weight, visit_rows, pulled, totals):
    pulled = pulled + jnp.dot(
        weight.astype(jnp.bfloat16), visit_rows, preferred_element_type=jnp.float32
    )
    return (pulled, totals + jnp.sum(weight, 1))


def local(emb, cluster):
    devices = lax.axis_size("blk")
    groups = devices // CYCLE
    doc_rows, width = emb.shape
    capacity = min(doc_rows // CYCLE, 3 * doc_rows // (2 * CYCLE * groups))
    slots = devices * capacity
    group_of = cluster // CL_CYCLE
    member = (group_of[:, None] == jnp.arange(groups, dtype=jnp.int32)[None, :]).astype(jnp.int32)
    running = jnp.cumsum(member, 0) - member
    place = jnp.sum(running * member, 1)
    target = place % CYCLE * groups + group_of
    slot_index = target * capacity + place // CYCLE
    send_rows = jnp.zeros((slots, width), jnp.bfloat16).at[slot_index].set(emb)
    send_ids = jnp.full((slots,), -1, jnp.int32).at[slot_index].set(cluster)
    got_rows, got_ids = (
        lax.all_to_all(
            send_rows.reshape(devices, capacity, width),
            "blk",
            split_axis=0,
            concat_axis=0,
            tiled=True,
        ),
        lax.all_to_all(
            send_ids.reshape(devices, capacity), "blk", split_axis=0, concat_axis=0, tiled=True
        ),
    )
    home_rows = got_rows.reshape(slots, width)
    home_ids = got_ids.reshape(slots)
    home_norm = squares(home_rows)
    pulled = jnp.zeros((slots, width), jnp.float32)
    totals = jnp.zeros((slots,), jnp.float32)
    weight = weights(home_rows, home_norm, home_ids, home_rows, home_ids, True)
    pulled, totals = absorb(weight, home_rows, pulled, totals)

    def advance(step, carry):
        visit_rows, visit_ids, pulled, totals = carry
        visit_rows, visit_ids = passed_along((visit_rows, visit_ids), "blk", groups)
        weight = weights(home_rows, home_norm, home_ids, visit_rows, visit_ids, False)
        pulled, totals = absorb(weight, visit_rows, pulled, totals)
        return (visit_rows, visit_ids, pulled, totals)

    _, _, pulled, totals = lax.fori_loop(1, CYCLE, advance, (home_rows, home_ids, pulled, totals))
    back_pulled, back_totals = (
        lax.all_to_all(
            pulled.reshape(devices, capacity, width), "blk", split_axis=0, concat_axis=0, tiled=True
        ),
        lax.all_to_all(
            totals.reshape(devices, capacity), "blk", split_axis=0, concat_axis=0, tiled=True
        ),
    )
    own_pulled = back_pulled.reshape(slots, width)[slot_index]
    own_totals = back_totals.reshape(slots)[slot_index]
    neighbour_mean = (own_pulled / (1.0 + own_totals)[:, None]).astype(jnp.bfloat16)
    dup_score = jnp.log(1.0 + own_totals)
    return (neighbour_mean, dup_score)


PIECES = 2
GATHER_DEVICES = 16
MESH = pl.DeviceIdType.MESH


def gather_kernel(emb_ref, cluster_ref, mean_ref, score_ref, docs, meta, ids_ref, pulled, totals,
                  load_sem, send_sem, recv_sem, meta_send, meta_recv):
    rows, width = emb_ref.shape
    piece = rows // PIECES
    me = lax.axis_index("blk")
    z, x, core = me // 4, (me // 2) % 2, me % 2
    z_end = GATHER_DEVICES // 4 - 1

    def slot_of(zz, xx, cc):
        return zz * 4 + xx * 2 + cc

    ways = ("up", "down", "x", "core")
    neighbour = {
        "up": slot_of(jnp.minimum(z + 1, z_end), x, core),
        "down": slot_of(jnp.maximum(z - 1, 0), x, core),
        "x": slot_of(z, 1 - x, core),
        "core": slot_of(z, x, 1 - core),
    }

    barrier = pltpu.get_barrier_semaphore()

    def greet(way):
        pl.semaphore_signal(
            barrier, inc=1, device_id={"blk": neighbour[way]}, device_id_type=MESH
        )

    pl.when(z > 0)(lambda: greet("down"))
    pl.when(z < z_end)(lambda: greet("up"))
    greet("x")
    greet("core")

    loads = [pltpu.make_async_copy(cluster_ref, ids_ref, load_sem.at[PIECES])]
    for h in range(PIECES):
        loads.append(
            pltpu.make_async_copy(
                emb_ref.at[pl.ds(h * piece, piece)], docs.at[me, h], load_sem.at[h]
            )
        )
    for load in loads:
        load.start()
    pulled[...] = jnp.zeros_like(pulled)
    totals[...] = jnp.zeros_like(totals)
    for load in loads:
        load.wait()

    own = docs[me].reshape(rows, width)
    own_f = own.astype(jnp.float32)
    own_norm = jnp.sum(own_f * own_f, 1, keepdims=True)
    line = lax.broadcasted_iota(jnp.int32, (rows, rows), 0)
    lane = lax.broadcasted_iota(jnp.int32, (rows, rows), 1)
    diagonal = line == lane
    ids_row = ids_ref[...].astype(jnp.float32)
    own_ids = jnp.sum(jnp.where(diagonal, ids_row, 0.0), 1, keepdims=True)
    norm_row = jnp.sum(jnp.where(diagonal, own_norm, 0.0), 0, keepdims=True)
    meta_line = lax.broadcasted_iota(jnp.int32, (8, rows), 0)
    meta[me] = jnp.where(meta_line == 0, norm_row, ids_row)

    pl.semaphore_wait(barrier, jnp.where((z > 0) & (z < z_end), 4, 3))

    sent = []

    def copy(way, slot, h, target):
        return pltpu.make_async_remote_copy(
            src_ref=docs.at[slot, h],
            dst_ref=docs.at[slot, h],
            send_sem=send_sem.at[way, slot, h],
            recv_sem=recv_sem.at[slot, h],
            device_id={"blk": target},
            device_id_type=MESH,
        )

    def meta_copy(way, slot, target):
        return pltpu.make_async_remote_copy(
            src_ref=meta.at[slot],
            dst_ref=meta.at[slot],
            send_sem=meta_send.at[way, slot],
            recv_sem=meta_recv.at[slot],
            device_id={"blk": target},
            device_id_type=MESH,
        )

    def send(pred, way, slot, h):
        index = ways.index(way)
        target = neighbour[way]

        def start():
            if h == PIECES - 1:
                meta_copy(index, slot, target).start()
            copy(index, slot, h, target).start()

        def finish():
            if h == PIECES - 1:
                meta_copy(index, slot, target).wait_send()
            copy(index, slot, h, target).wait_send()

        pl.when(pred)(start)
        sent.append(lambda: pl.when(pred)(finish))

    def arrive(slot, h):
        if h == PIECES - 1:
            meta_copy(3, slot, neighbour["core"]).wait_recv()
        copy(3, slot, h, neighbour["core"]).wait_recv()

    def to_line(zz, h):
        slot = slot_of(zz, x, core)
        send((zz >= z) & (z > 0), "down", slot, h)
        send((zz <= z) & (z < z_end), "up", slot, h)

    def to_side(zz, h):
        from_low, from_high = (zz == 0) & (z > 0), (zz == z_end) & (z < z_end)
        if h >= PIECES // 2:
            from_low = from_low & (z == 1)
            from_high = from_high & (z == z_end - 1)
        send(jnp.logical_not(from_low | from_high), "x", slot_of(zz, x, core), h)

    def to_core(zz, xx, h):
        send(z >= 0, "core", slot_of(zz, xx, core), h)

    def pass_column(zz, h):
        arrive(slot_of(zz, x, core), h)
        to_line(zz, h)
        to_side(zz, h)
        to_core(zz, x, h)

    def pass_other(zz, h):
        slot = slot_of(zz, 1 - x, core)
        arrive(slot, h)
        up, down = zz == 0, zz == z_end
        if h >= PIECES // 2:
            up, down = up & (z == 0), down & (z == z_end)
        send(down & (z > 0), "down", slot, h)
        send(up & (z < z_end), "up", slot, h)
        to_core(zz, 1 - x, h)

    def absorb(zz, xx, own_chip=False):
        for h in range(PIECES):
            arrive(slot_of(zz, xx, 1 - core), h)
        first = slot_of(zz, xx, 0)
        visit = docs[pl.ds(first, 2)].reshape(2 * rows, width)
        info = meta[pl.ds(first, 2)]
        visit_norm = jnp.concatenate([info[0, 0:1], info[1, 0:1]], 1)
        visit_ids = jnp.concatenate([info[0, 1:2], info[1, 1:2]], 1)
        inner = lax.dot_general(
            docs[me].reshape(rows, width),
            visit,
            (((1,), (1,)), ((), ())),
            preferred_element_type=jnp.float32,
        )
        distance = jnp.maximum(own_norm + visit_norm - 2.0 * inner, 0.0)
        allowed = own_ids == visit_ids
        if own_chip:
            home = lax.broadcasted_iota(jnp.int32, (rows, 2 * rows), 0) + core * rows
            away = lax.broadcasted_iota(jnp.int32, (rows, 2 * rows), 1)
            allowed = allowed & (home != away)
        weight = jnp.where(allowed, jnp.exp(distance * (-SHARPNESS / width)), 0.0)
        totals[...] += jnp.sum(weight, 1, keepdims=True)
        pulled[...] += jnp.dot(
            weight.astype(jnp.bfloat16), visit, preferred_element_type=jnp.float32
        )

    z1 = jnp.where(z % 2 == 0, 1, 2)
    z3 = jnp.where(z < 2, z_end, 0)
    z2 = 6 - z - z1 - z3
    early = range(PIECES // 2)
    late = range(PIECES // 2, PIECES)

    def column(zz, pieces):
        for h in pieces:
            pass_column(zz, h)

    def other(zz, pieces):
        for h in pieces:
            pass_other(zz, h)

    def begin():
        for h in (*late, *early):
            to_line(z, h)
        for h in (*early, *late):
            to_side(z, h)
        for h in (*late, *early):
            to_core(z, x, h)
        absorb(z, x, True)

    def at_end():
        begin()
        column(z1, (*late, *early))
        other(z, (*early, *late))
        absorb(z1, x)
        column(z2, (*late, *early))
        other(z1, (*late, *early))
        absorb(z, 1 - x)
        absorb(z2, x)
        column(z3, late)
        absorb(z1, 1 - x)
        other(z2, (*late, *early))
        column(z3, early)
        absorb(z2, 1 - x)
        absorb(z3, x)
        other(z3, (*late, *early))
        absorb(z3, 1 - x)
        close()

    def at_middle():
        begin()
        column(z1, (*late, *early))
        column(z2, (*late, *early))
        other(z, (*early, *late))
        absorb(z1, x)
        other(z2, early)
        column(z3, late)
        absorb(z2, x)
        column(z3, early)
        other(z1, (*late, *early))
        other(z2, late)
        absorb(z, 1 - x)
        other(z3, early)
        absorb(z1, 1 - x)
        absorb(z3, x)
        absorb(z2, 1 - x)
        other(z3, late)
        absorb(z3, 1 - x)
        close()

    def close():
        scale = 1.0 + totals[...]
        mean_ref[...] = (pulled[...] / scale).astype(jnp.bfloat16)
        score_ref[...] = jnp.sum(jnp.where(diagonal, jnp.log(scale), 0.0), 0, keepdims=True)
        for finish in sent:
            finish()
        sent.clear()

    middle = (z > 0) & (z < z_end)
    pl.when(middle)(at_middle)
    pl.when(jnp.logical_not(middle))(at_end)


def gathered(emb, cluster):
    rows, width = emb.shape
    devices = GATHER_DEVICES
    vmem = pl.BlockSpec(memory_space=pltpu.VMEM)
    mean, score = pl.pallas_call(
        gather_kernel,
        out_shape=(
            jax.ShapeDtypeStruct((rows, width), jnp.bfloat16),
            jax.ShapeDtypeStruct((1, rows), jnp.float32),
        ),
        in_specs=[pl.BlockSpec(memory_space=pl.ANY)] * 2,
        out_specs=(vmem, vmem),
        scratch_shapes=[
            pltpu.VMEM((devices, PIECES, rows // PIECES, width), jnp.bfloat16),
            pltpu.VMEM((devices, 8, rows), jnp.float32),
            pltpu.VMEM((1, rows), jnp.int32),
            pltpu.VMEM((rows, width), jnp.float32),
            pltpu.VMEM((rows, 1), jnp.float32),
            pltpu.SemaphoreType.DMA((PIECES + 1,)),
            pltpu.SemaphoreType.DMA((4, devices, PIECES)),
            pltpu.SemaphoreType.DMA((devices, PIECES)),
            pltpu.SemaphoreType.DMA((4, devices)),
            pltpu.SemaphoreType.DMA((devices,)),
        ],
        compiler_params=pltpu.CompilerParams(
            collective_id=0, has_side_effects=True, vmem_limit_bytes=40 << 20
        ),
        cost_estimate=pl.CostEstimate(
            flops=4 * devices * rows * rows * width,
            bytes_accessed=4 * rows * width,
            transcendentals=devices * rows * rows,
        ),
    )(emb, cluster.reshape(1, rows))
    return mean, score.reshape(rows)


def solution(mesh):
    small = mesh.shape["blk"] == GATHER_DEVICES
    return jax.shard_map(
        gathered if small else local,
        mesh=mesh,
        in_specs=(P(("parts", "blk"), None), P(("parts", "blk"))),
        out_specs=(P(("parts", "blk"), None), P(("parts", "blk"))),
        check_vma=False,
    )
```

```python
import jax
import jax.numpy as jnp
from jax import lax
from jax.experimental import pallas as pl
from jax.experimental.pallas import tpu as pltpu
from jax.sharding import PartitionSpec as P

CYCLE = 16
CL_CYCLE = 4


SHARPNESS = 2.0


def passed_along(block, axis, distance):
    devices = range(lax.axis_size(axis))
    route = [((i - distance) % len(devices), i) for i in devices]
    return lax.ppermute(block, axis, route)


def squares(rows):
    return jnp.sum(jnp.square(rows.astype(jnp.float32)), 1)


def weights(home_rows, home_norm, home_ids, visit_rows, visit_ids, skip_self):
    visit_norm = squares(visit_rows)
    inner = lax.dot_general(
        home_rows, visit_rows, (((1,), (1,)), ((), ())), preferred_element_type=jnp.float32
    )
    distance = jnp.maximum(home_norm[:, None] + visit_norm[None, :] - 2.0 * inner, 0.0)
    allowed = (home_ids[:, None] == visit_ids[None, :]) & (home_ids[:, None] >= 0)
    if skip_self:
        row_pos = jnp.arange(home_rows.shape[0], dtype=jnp.int32)
        allowed = allowed & (row_pos[:, None] != row_pos[None, :])
    return jnp.where(allowed, jnp.exp(-SHARPNESS * distance / home_rows.shape[1]), 0.0)


def absorb(weight, visit_rows, pulled, totals):
    pulled = pulled + jnp.dot(
        weight.astype(jnp.bfloat16), visit_rows, preferred_element_type=jnp.float32
    )
    return (pulled, totals + jnp.sum(weight, 1))


def local(emb, cluster):
    devices = lax.axis_size("blk")
    groups = devices // CYCLE
    doc_rows, width = emb.shape
    capacity = min(doc_rows // CYCLE, 3 * doc_rows // (2 * CYCLE * groups))
    slots = devices * capacity
    group_of = cluster // CL_CYCLE
    member = (group_of[:, None] == jnp.arange(groups, dtype=jnp.int32)[None, :]).astype(jnp.int32)
    running = jnp.cumsum(member, 0) - member
    place = jnp.sum(running * member, 1)
    target = place % CYCLE * groups + group_of
    slot_index = target * capacity + place // CYCLE
    send_rows = jnp.zeros((slots, width), jnp.bfloat16).at[slot_index].set(emb)
    send_ids = jnp.full((slots,), -1, jnp.int32).at[slot_index].set(cluster)
    got_rows, got_ids = (
        lax.all_to_all(
            send_rows.reshape(devices, capacity, width),
            "blk",
            split_axis=0,
            concat_axis=0,
            tiled=True,
        ),
        lax.all_to_all(
            send_ids.reshape(devices, capacity), "blk", split_axis=0, concat_axis=0, tiled=True
        ),
    )
    home_rows = got_rows.reshape(slots, width)
    home_ids = got_ids.reshape(slots)
    home_norm = squares(home_rows)
    pulled = jnp.zeros((slots, width), jnp.float32)
    totals = jnp.zeros((slots,), jnp.float32)
    weight = weights(home_rows, home_norm, home_ids, home_rows, home_ids, True)
    pulled, totals = absorb(weight, home_rows, pulled, totals)

    def advance(step, carry):
        visit_rows, visit_ids, pulled, totals = carry
        visit_rows, visit_ids = passed_along((visit_rows, visit_ids), "blk", groups)
        weight = weights(home_rows, home_norm, home_ids, visit_rows, visit_ids, False)
        pulled, totals = absorb(weight, visit_rows, pulled, totals)
        return (visit_rows, visit_ids, pulled, totals)

    _, _, pulled, totals = lax.fori_loop(1, CYCLE, advance, (home_rows, home_ids, pulled, totals))
    back_pulled, back_totals = (
        lax.all_to_all(
            pulled.reshape(devices, capacity, width), "blk", split_axis=0, concat_axis=0, tiled=True
        ),
        lax.all_to_all(
            totals.reshape(devices, capacity), "blk", split_axis=0, concat_axis=0, tiled=True
        ),
    )
    own_pulled = back_pulled.reshape(slots, width)[slot_index]
    own_totals = back_totals.reshape(slots)[slot_index]
    neighbour_mean = (own_pulled / (1.0 + own_totals)[:, None]).astype(jnp.bfloat16)
    dup_score = jnp.log(1.0 + own_totals)
    return (neighbour_mean, dup_score)


PIECES = 2
GATHER_DEVICES = 16
MESH = pl.DeviceIdType.MESH


def gather_kernel(emb_ref, cluster_ref, mean_ref, score_ref, docs, meta, ids_ref, pulled, totals,
                  load_sem, send_sem, recv_sem, meta_send, meta_recv):
    rows, width = emb_ref.shape
    piece = rows // PIECES
    me = lax.axis_index("blk")
    z, x, core = me // 4, (me // 2) % 2, me % 2
    z_end = GATHER_DEVICES // 4 - 1

    def slot_of(zz, xx, cc):
        return zz * 4 + xx * 2 + cc

    ways = ("up", "down", "x", "core")
    neighbour = {
        "up": slot_of(jnp.minimum(z + 1, z_end), x, core),
        "down": slot_of(jnp.maximum(z - 1, 0), x, core),
        "x": slot_of(z, 1 - x, core),
        "core": slot_of(z, x, 1 - core),
    }

    barrier = pltpu.get_barrier_semaphore()

    def greet(way):
        pl.semaphore_signal(
            barrier, inc=1, device_id={"blk": neighbour[way]}, device_id_type=MESH
        )

    pl.when(z > 0)(lambda: greet("down"))
    pl.when(z < z_end)(lambda: greet("up"))
    greet("x")
    greet("core")

    loads = [pltpu.make_async_copy(cluster_ref, ids_ref, load_sem.at[PIECES])]
    for h in range(PIECES):
        loads.append(
            pltpu.make_async_copy(
                emb_ref.at[pl.ds(h * piece, piece)], docs.at[me, h], load_sem.at[h]
            )
        )
    for load in loads:
        load.start()
    pulled[...] = jnp.zeros_like(pulled)
    totals[...] = jnp.zeros_like(totals)
    for load in loads:
        load.wait()

    own = docs[me].reshape(rows, width)
    own_f = own.astype(jnp.float32)
    own_norm = jnp.sum(own_f * own_f, 1, keepdims=True)
    line = lax.broadcasted_iota(jnp.int32, (rows, rows), 0)
    lane = lax.broadcasted_iota(jnp.int32, (rows, rows), 1)
    diagonal = line == lane
    ids_row = ids_ref[...].astype(jnp.float32)
    own_ids = jnp.sum(jnp.where(diagonal, ids_row, 0.0), 1, keepdims=True)
    norm_row = jnp.sum(jnp.where(diagonal, own_norm, 0.0), 0, keepdims=True)
    meta_line = lax.broadcasted_iota(jnp.int32, (8, rows), 0)
    meta[me] = jnp.where(meta_line == 0, norm_row, ids_row)

    pl.semaphore_wait(barrier, jnp.where((z > 0) & (z < z_end), 4, 3))

    sent = []

    def copy(way, slot, h, target):
        return pltpu.make_async_remote_copy(
            src_ref=docs.at[slot, h],
            dst_ref=docs.at[slot, h],
            send_sem=send_sem.at[way, slot, h],
            recv_sem=recv_sem.at[slot, h],
            device_id={"blk": target},
            device_id_type=MESH,
        )

    def meta_copy(way, slot, target):
        return pltpu.make_async_remote_copy(
            src_ref=meta.at[slot],
            dst_ref=meta.at[slot],
            send_sem=meta_send.at[way, slot],
            recv_sem=meta_recv.at[slot],
            device_id={"blk": target},
            device_id_type=MESH,
        )

    def send(pred, way, slot, h):
        index = ways.index(way)
        target = neighbour[way]

        def start():
            if h == PIECES - 1:
                meta_copy(index, slot, target).start()
            copy(index, slot, h, target).start()

        def finish():
            if h == PIECES - 1:
                meta_copy(index, slot, target).wait_send()
            copy(index, slot, h, target).wait_send()

        pl.when(pred)(start)
        sent.append(lambda: pl.when(pred)(finish))

    def arrive(slot, h):
        if h == PIECES - 1:
            meta_copy(3, slot, neighbour["core"]).wait_recv()
        copy(3, slot, h, neighbour["core"]).wait_recv()

    def to_line(zz, h):
        slot = slot_of(zz, x, core)
        send((zz >= z) & (z > 0), "down", slot, h)
        send((zz <= z) & (z < z_end), "up", slot, h)

    def to_side(zz, h):
        from_low, from_high = (zz == 0) & (z > 0), (zz == z_end) & (z < z_end)
        if h >= PIECES // 2:
            from_low = from_low & (z == 1)
            from_high = from_high & (z == z_end - 1)
        send(jnp.logical_not(from_low | from_high), "x", slot_of(zz, x, core), h)

    def to_core(zz, xx, h):
        send(z >= 0, "core", slot_of(zz, xx, core), h)

    def pass_column(zz, h):
        arrive(slot_of(zz, x, core), h)
        to_line(zz, h)
        to_side(zz, h)
        to_core(zz, x, h)

    def pass_other(zz, h):
        slot = slot_of(zz, 1 - x, core)
        arrive(slot, h)
        up, down = zz == 0, zz == z_end
        if h >= PIECES // 2:
            up, down = up & (z == 0), down & (z == z_end)
        send(down & (z > 0), "down", slot, h)
        send(up & (z < z_end), "up", slot, h)
        to_core(zz, 1 - x, h)

    def absorb(zz, xx, own_chip=False):
        for h in range(PIECES):
            arrive(slot_of(zz, xx, 1 - core), h)
        first = slot_of(zz, xx, 0)
        visit = docs[pl.ds(first, 2)].reshape(2 * rows, width)
        info = meta[pl.ds(first, 2)]
        visit_norm = jnp.concatenate([info[0, 0:1], info[1, 0:1]], 1)
        visit_ids = jnp.concatenate([info[0, 1:2], info[1, 1:2]], 1)
        inner = lax.dot_general(
            docs[me].reshape(rows, width),
            visit,
            (((1,), (1,)), ((), ())),
            preferred_element_type=jnp.float32,
        )
        distance = jnp.maximum(own_norm + visit_norm - 2.0 * inner, 0.0)
        allowed = own_ids == visit_ids
        if own_chip:
            home = lax.broadcasted_iota(jnp.int32, (rows, 2 * rows), 0) + core * rows
            away = lax.broadcasted_iota(jnp.int32, (rows, 2 * rows), 1)
            allowed = allowed & (home != away)
        weight = jnp.where(allowed, jnp.exp(distance * (-SHARPNESS / width)), 0.0)
        totals[...] += jnp.sum(weight, 1, keepdims=True)
        pulled[...] += jnp.dot(
            weight.astype(jnp.bfloat16), visit, preferred_element_type=jnp.float32
        )

    z1 = jnp.where(z % 2 == 0, 1, 2)
    z3 = jnp.where(z < 2, z_end, 0)
    z2 = 6 - z - z1 - z3
    early = range(PIECES // 2)
    late = range(PIECES // 2, PIECES)

    def column(zz, pieces):
        for h in pieces:
            pass_column(zz, h)

    def other(zz, pieces):
        for h in pieces:
            pass_other(zz, h)

    def begin():
        for h in (*late, *early):
            to_line(z, h)
        for h in (*early, *late):
            to_side(z, h)
        for h in (*late, *early):
            to_core(z, x, h)
        absorb(z, x, True)

    def at_end():
        begin()
        column(z1, (*late, *early))
        other(z, (*early, *late))
        absorb(z1, x)
        column(z2, (*late, *early))
        other(z1, (*late, *early))
        absorb(z, 1 - x)
        absorb(z2, x)
        column(z3, late)
        absorb(z1, 1 - x)
        other(z2, (*late, *early))
        column(z3, early)
        absorb(z2, 1 - x)
        absorb(z3, x)
        other(z3, (*late, *early))
        absorb(z3, 1 - x)
        close()

    def at_middle():
        begin()
        column(z1, (*late, *early))
        column(z2, (*late, *early))
        other(z, (*early, *late))
        absorb(z1, x)
        other(z2, early)
        column(z3, late)
        absorb(z2, x)
        column(z3, early)
        other(z1, (*late, *early))
        other(z2, late)
        absorb(z, 1 - x)
        other(z3, early)
        absorb(z1, 1 - x)
        absorb(z3, x)
        absorb(z2, 1 - x)
        other(z3, late)
        absorb(z3, 1 - x)
        close()

    def close():
        scale = 1.0 + totals[...]
        mean_ref[...] = (pulled[...] / scale).astype(jnp.bfloat16)
        score_ref[...] = jnp.sum(jnp.where(diagonal, jnp.log(scale), 0.0), 0, keepdims=True)
        for finish in sent:
            finish()
        sent.clear()

    middle = (z > 0) & (z < z_end)
    pl.when(middle)(at_middle)
    pl.when(jnp.logical_not(middle))(at_end)


def gathered(emb, cluster):
    rows, width = emb.shape
    devices = GATHER_DEVICES
    vmem = pl.BlockSpec(memory_space=pltpu.VMEM)
    mean, score = pl.pallas_call(
        gather_kernel,
        out_shape=(
            jax.ShapeDtypeStruct((rows, width), jnp.bfloat16),
            jax.ShapeDtypeStruct((1, rows), jnp.float32),
        ),
        in_specs=[pl.BlockSpec(memory_space=pl.ANY)] * 2,
        out_specs=(vmem, vmem),
        scratch_shapes=[
            pltpu.VMEM((devices, PIECES, rows // PIECES, width), jnp.bfloat16),
            pltpu.VMEM((devices, 8, rows), jnp.float32),
            pltpu.VMEM((1, rows), jnp.int32),
            pltpu.VMEM((rows, width), jnp.float32),
            pltpu.VMEM((rows, 1), jnp.float32),
            pltpu.SemaphoreType.DMA((PIECES + 1,)),
            pltpu.SemaphoreType.DMA((4, devices, PIECES)),
            pltpu.SemaphoreType.DMA((devices, PIECES)),
            pltpu.SemaphoreType.DMA((4, devices)),
            pltpu.SemaphoreType.DMA((devices,)),
        ],
        compiler_params=pltpu.CompilerParams(
            collective_id=0, has_side_effects=True, vmem_limit_bytes=107 << 19
        ),
        cost_estimate=pl.CostEstimate(
            flops=4 * devices * rows * rows * width,
            bytes_accessed=4 * rows * width,
            transcendentals=devices * rows * rows,
        ),
    )(emb, cluster.reshape(1, rows))
    return mean, score.reshape(rows)


def solution(mesh):
    small = mesh.shape["blk"] == GATHER_DEVICES
    return jax.shard_map(
        gathered if small else local,
        mesh=mesh,
        in_specs=(P(("parts", "blk"), None), P(("parts", "blk"))),
        out_specs=(P(("parts", "blk"), None), P(("parts", "blk"))),
        check_vma=False,
    )
```

```python
import jax
import jax.numpy as jnp
from jax import lax
from jax.experimental import pallas as pl
from jax.experimental.pallas import tpu as pltpu
from jax.sharding import PartitionSpec as P

CYCLE = 16
CL_CYCLE = 4


SHARPNESS = 2.0


def passed_along(block, axis, distance):
    devices = range(lax.axis_size(axis))
    route = [((i - distance) % len(devices), i) for i in devices]
    return lax.ppermute(block, axis, route)


def squares(rows):
    return jnp.sum(jnp.square(rows.astype(jnp.float32)), 1)


def weights(home_rows, home_norm, home_ids, visit_rows, visit_ids, skip_self):
    visit_norm = squares(visit_rows)
    inner = lax.dot_general(
        home_rows, visit_rows, (((1,), (1,)), ((), ())), preferred_element_type=jnp.float32
    )
    distance = jnp.maximum(home_norm[:, None] + visit_norm[None, :] - 2.0 * inner, 0.0)
    allowed = (home_ids[:, None] == visit_ids[None, :]) & (home_ids[:, None] >= 0)
    if skip_self:
        row_pos = jnp.arange(home_rows.shape[0], dtype=jnp.int32)
        allowed = allowed & (row_pos[:, None] != row_pos[None, :])
    return jnp.where(allowed, jnp.exp(-SHARPNESS * distance / home_rows.shape[1]), 0.0)


def absorb(weight, visit_rows, pulled, totals):
    pulled = pulled + jnp.dot(
        weight.astype(jnp.bfloat16), visit_rows, preferred_element_type=jnp.float32
    )
    return (pulled, totals + jnp.sum(weight, 1))


def local(emb, cluster):
    devices = lax.axis_size("blk")
    groups = devices // CYCLE
    doc_rows, width = emb.shape
    capacity = min(doc_rows // CYCLE, 3 * doc_rows // (2 * CYCLE * groups))
    slots = devices * capacity
    group_of = cluster // CL_CYCLE
    member = (group_of[:, None] == jnp.arange(groups, dtype=jnp.int32)[None, :]).astype(jnp.int32)
    running = jnp.cumsum(member, 0) - member
    place = jnp.sum(running * member, 1)
    target = place % CYCLE * groups + group_of
    slot_index = target * capacity + place // CYCLE
    send_rows = jnp.zeros((slots, width), jnp.bfloat16).at[slot_index].set(emb)
    send_ids = jnp.full((slots,), -1, jnp.int32).at[slot_index].set(cluster)
    got_rows, got_ids = (
        lax.all_to_all(
            send_rows.reshape(devices, capacity, width),
            "blk",
            split_axis=0,
            concat_axis=0,
            tiled=True,
        ),
        lax.all_to_all(
            send_ids.reshape(devices, capacity), "blk", split_axis=0, concat_axis=0, tiled=True
        ),
    )
    home_rows = got_rows.reshape(slots, width)
    home_ids = got_ids.reshape(slots)
    home_norm = squares(home_rows)
    pulled = jnp.zeros((slots, width), jnp.float32)
    totals = jnp.zeros((slots,), jnp.float32)
    weight = weights(home_rows, home_norm, home_ids, home_rows, home_ids, True)
    pulled, totals = absorb(weight, home_rows, pulled, totals)

    def advance(step, carry):
        visit_rows, visit_ids, pulled, totals = carry
        visit_rows, visit_ids = passed_along((visit_rows, visit_ids), "blk", groups)
        weight = weights(home_rows, home_norm, home_ids, visit_rows, visit_ids, False)
        pulled, totals = absorb(weight, visit_rows, pulled, totals)
        return (visit_rows, visit_ids, pulled, totals)

    _, _, pulled, totals = lax.fori_loop(1, CYCLE, advance, (home_rows, home_ids, pulled, totals))
    back_pulled, back_totals = (
        lax.all_to_all(
            pulled.reshape(devices, capacity, width), "blk", split_axis=0, concat_axis=0, tiled=True
        ),
        lax.all_to_all(
            totals.reshape(devices, capacity), "blk", split_axis=0, concat_axis=0, tiled=True
        ),
    )
    own_pulled = back_pulled.reshape(slots, width)[slot_index]
    own_totals = back_totals.reshape(slots)[slot_index]
    neighbour_mean = (own_pulled / (1.0 + own_totals)[:, None]).astype(jnp.bfloat16)
    dup_score = jnp.log(1.0 + own_totals)
    return (neighbour_mean, dup_score)


PIECES = 2
GATHER_DEVICES = 16
MESH = pl.DeviceIdType.MESH


def gather_kernel(emb_ref, cluster_ref, mean_ref, score_ref, docs, meta, ids_ref, pulled, totals,
                  load_sem, send_sem, recv_sem, meta_send, meta_recv):
    rows, width = emb_ref.shape
    piece = rows // PIECES
    me = lax.axis_index("blk")
    z, x, core = me // 4, (me // 2) % 2, me % 2
    z_end = GATHER_DEVICES // 4 - 1

    def slot_of(zz, xx, cc):
        return zz * 4 + xx * 2 + cc

    ways = ("up", "down", "x", "core")
    neighbour = {
        "up": slot_of(jnp.minimum(z + 1, z_end), x, core),
        "down": slot_of(jnp.maximum(z - 1, 0), x, core),
        "x": slot_of(z, 1 - x, core),
        "core": slot_of(z, x, 1 - core),
    }

    barrier = pltpu.get_barrier_semaphore()

    def greet(way):
        pl.semaphore_signal(
            barrier, inc=1, device_id={"blk": neighbour[way]}, device_id_type=MESH
        )

    pl.when(z > 0)(lambda: greet("down"))
    pl.when(z < z_end)(lambda: greet("up"))
    greet("x")
    greet("core")

    loads = [pltpu.make_async_copy(cluster_ref, ids_ref, load_sem.at[PIECES])]
    for h in range(PIECES):
        loads.append(
            pltpu.make_async_copy(
                emb_ref.at[pl.ds(h * piece, piece)], docs.at[me, h], load_sem.at[h]
            )
        )
    for load in loads:
        load.start()
    pulled[...] = jnp.zeros_like(pulled)
    totals[...] = jnp.zeros_like(totals)
    for load in loads:
        load.wait()

    own = docs[me].reshape(rows, width)
    own_f = own.astype(jnp.float32)
    own_norm = jnp.sum(own_f * own_f, 1, keepdims=True)
    line = lax.broadcasted_iota(jnp.int32, (rows, rows), 0)
    lane = lax.broadcasted_iota(jnp.int32, (rows, rows), 1)
    diagonal = line == lane
    ids_row = ids_ref[...].astype(jnp.float32)
    own_ids = jnp.sum(jnp.where(diagonal, ids_row, 0.0), 1, keepdims=True)
    norm_row = jnp.sum(jnp.where(diagonal, own_norm, 0.0), 0, keepdims=True)
    meta_line = lax.broadcasted_iota(jnp.int32, (8, rows), 0)
    meta[me] = jnp.where(meta_line == 0, norm_row, ids_row)

    pl.semaphore_wait(barrier, jnp.where((z > 0) & (z < z_end), 4, 3))

    sent = []

    def copy(way, slot, h, target):
        return pltpu.make_async_remote_copy(
            src_ref=docs.at[slot, h],
            dst_ref=docs.at[slot, h],
            send_sem=send_sem.at[way, slot // 2, h],
            recv_sem=recv_sem.at[slot, h],
            device_id={"blk": target},
            device_id_type=MESH,
        )

    def meta_copy(way, slot, target):
        return pltpu.make_async_remote_copy(
            src_ref=meta.at[slot],
            dst_ref=meta.at[slot],
            send_sem=meta_send.at[way, slot // 2],
            recv_sem=meta_recv.at[slot],
            device_id={"blk": target},
            device_id_type=MESH,
        )

    def send(pred, way, slot, h):
        index = ways.index(way)
        target = neighbour[way]

        def start():
            if h == PIECES - 1:
                meta_copy(index, slot, target).start()
            copy(index, slot, h, target).start()

        def finish():
            if h == PIECES - 1:
                meta_copy(index, slot, target).wait_send()
            copy(index, slot, h, target).wait_send()

        pl.when(pred)(start)
        sent.append(lambda: pl.when(pred)(finish))

    def arrive(slot, h):
        if h == PIECES - 1:
            meta_copy(3, slot, neighbour["core"]).wait_recv()
        copy(3, slot, h, neighbour["core"]).wait_recv()

    def to_line(zz, h):
        slot = slot_of(zz, x, core)
        send((zz >= z) & (z > 0), "down", slot, h)
        send((zz <= z) & (z < z_end), "up", slot, h)

    def to_side(zz, h):
        from_low, from_high = (zz == 0) & (z > 0), (zz == z_end) & (z < z_end)
        if h >= PIECES // 2:
            from_low = from_low & (z == 1)
            from_high = from_high & (z == z_end - 1)
        send(jnp.logical_not(from_low | from_high), "x", slot_of(zz, x, core), h)

    def to_core(zz, xx, h):
        send(z >= 0, "core", slot_of(zz, xx, core), h)

    def pass_column(zz, h):
        arrive(slot_of(zz, x, core), h)
        to_line(zz, h)
        to_side(zz, h)
        to_core(zz, x, h)

    def pass_other(zz, h):
        slot = slot_of(zz, 1 - x, core)
        arrive(slot, h)
        up, down = zz == 0, zz == z_end
        if h >= PIECES // 2:
            up, down = up & (z == 0), down & (z == z_end)
        send(down & (z > 0), "down", slot, h)
        send(up & (z < z_end), "up", slot, h)
        to_core(zz, 1 - x, h)

    def absorb(zz, xx, own_chip=False):
        for h in range(PIECES):
            arrive(slot_of(zz, xx, 1 - core), h)
        first = slot_of(zz, xx, 0)
        visit = docs[pl.ds(first, 2)].reshape(2 * rows, width)
        info = meta[pl.ds(first, 2)]
        visit_norm = jnp.concatenate([info[0, 0:1], info[1, 0:1]], 1)
        visit_ids = jnp.concatenate([info[0, 1:2], info[1, 1:2]], 1)
        inner = lax.dot_general(
            docs[me].reshape(rows, width),
            visit,
            (((1,), (1,)), ((), ())),
            preferred_element_type=jnp.float32,
        )
        distance = jnp.maximum(own_norm + visit_norm - 2.0 * inner, 0.0)
        allowed = own_ids == visit_ids
        if own_chip:
            home = lax.broadcasted_iota(jnp.int32, (rows, 2 * rows), 0) + core * rows
            away = lax.broadcasted_iota(jnp.int32, (rows, 2 * rows), 1)
            allowed = allowed & (home != away)
        weight = jnp.where(allowed, jnp.exp(distance * (-SHARPNESS / width)), 0.0)
        totals[...] += jnp.sum(weight, 1, keepdims=True)
        pulled[...] += jnp.dot(
            weight.astype(jnp.bfloat16), visit, preferred_element_type=jnp.float32
        )

    z1 = jnp.where(z % 2 == 0, 1, 2)
    z3 = jnp.where(z < 2, z_end, 0)
    z2 = 6 - z - z1 - z3
    early = range(PIECES // 2)
    late = range(PIECES // 2, PIECES)

    def column(zz, pieces):
        for h in pieces:
            pass_column(zz, h)

    def other(zz, pieces):
        for h in pieces:
            pass_other(zz, h)

    def begin():
        for h in (*late, *early):
            to_line(z, h)
        for h in (*early, *late):
            to_side(z, h)
        for h in (*late, *early):
            to_core(z, x, h)
        absorb(z, x, True)

    def at_end():
        begin()
        column(z1, (*late, *early))
        other(z, (*early, *late))
        absorb(z1, x)
        column(z2, (*late, *early))
        other(z1, (*late, *early))
        absorb(z, 1 - x)
        absorb(z2, x)
        column(z3, late)
        absorb(z1, 1 - x)
        other(z2, (*late, *early))
        column(z3, early)
        absorb(z2, 1 - x)
        absorb(z3, x)
        other(z3, (*late, *early))
        absorb(z3, 1 - x)
        close()

    def at_middle():
        begin()
        column(z1, (*late, *early))
        column(z2, (*late, *early))
        other(z, (*early, *late))
        absorb(z1, x)
        other(z2, early)
        column(z3, late)
        absorb(z2, x)
        column(z3, early)
        other(z1, (*late, *early))
        other(z2, late)
        absorb(z, 1 - x)
        other(z3, early)
        absorb(z1, 1 - x)
        absorb(z3, x)
        absorb(z2, 1 - x)
        other(z3, late)
        absorb(z3, 1 - x)
        close()

    def close():
        scale = 1.0 + totals[...]
        mean_ref[...] = (pulled[...] / scale).astype(jnp.bfloat16)
        score_ref[...] = jnp.sum(jnp.where(diagonal, jnp.log(scale), 0.0), 0, keepdims=True)
        for finish in sent:
            finish()
        sent.clear()

    middle = (z > 0) & (z < z_end)
    pl.when(middle)(at_middle)
    pl.when(jnp.logical_not(middle))(at_end)


def gathered(emb, cluster):
    rows, width = emb.shape
    devices = GATHER_DEVICES
    vmem = pl.BlockSpec(memory_space=pltpu.VMEM)
    mean, score = pl.pallas_call(
        gather_kernel,
        out_shape=(
            jax.ShapeDtypeStruct((rows, width), jnp.bfloat16),
            jax.ShapeDtypeStruct((1, rows), jnp.float32),
        ),
        in_specs=[pl.BlockSpec(memory_space=pl.ANY)] * 2,
        out_specs=(vmem, vmem),
        scratch_shapes=[
            pltpu.VMEM((devices, PIECES, rows // PIECES, width), jnp.bfloat16),
            pltpu.VMEM((devices, 8, rows), jnp.float32),
            pltpu.VMEM((1, rows), jnp.int32),
            pltpu.VMEM((rows, width), jnp.float32),
            pltpu.VMEM((rows, 1), jnp.float32),
            pltpu.SemaphoreType.DMA((PIECES + 1,)),
            pltpu.SemaphoreType.DMA((4, devices // 2, PIECES)),
            pltpu.SemaphoreType.DMA((devices, PIECES)),
            pltpu.SemaphoreType.DMA((4, devices // 2)),
            pltpu.SemaphoreType.DMA((devices,)),
        ],
        compiler_params=pltpu.CompilerParams(
            collective_id=0, has_side_effects=True, vmem_limit_bytes=107 << 19
        ),
        cost_estimate=pl.CostEstimate(
            flops=4 * devices * rows * rows * width,
            bytes_accessed=4 * rows * width,
            transcendentals=devices * rows * rows,
        ),
    )(emb, cluster.reshape(1, rows))
    return mean, score.reshape(rows)


def solution(mesh):
    small = mesh.shape["blk"] == GATHER_DEVICES
    return jax.shard_map(
        gathered if small else local,
        mesh=mesh,
        in_specs=(P(("parts", "blk"), None), P(("parts", "blk"))),
        out_specs=(P(("parts", "blk"), None), P(("parts", "blk"))),
        check_vma=False,
    )
```
